32 devices in a mesh: group: 4 (over y, core), member: 8 (over z, x).
Axes of the slice: x: 2, y: 2, z: 4, core: 2. Of those that a mesh axis runs over, the one named last changes fastest.
Arguments:
- candidates: bfloat16 [512, 32, 1024], P('member', 'group'), may hold values from -6 to 6
- kv_cache: bfloat16 [32, 2048, 2048], P('group', 'member'), may hold values from -6 to 6
- cache_request: int32 [32], replicated, may hold values from 0 to 31, as said below
- rank_request: int32 [32], replicated, may hold values from 0 to 31, as said below
- hist_blocks: int32 [32], replicated, may hold values from 1 to 16, 272 in all
- w_uq: bfloat16 [1024, 2048], replicated, may hold values from -0.1875 to 0.1875
- w_out: bfloat16 [1024, 1024], replicated, may hold values from -0.1875 to 0.1875
Outputs:
- ranked: bfloat16 [512, 32, 1024], P('member', 'group')
The draws below stay inside these ranges and needn't reach their ends.
Inputs may be any that keep to these rules, and one draw needn't show every extreme that they name: `cache_request`: A permutation; cache row q lies on group q // 8, events split over member. `rank_request`: A permutation; group g ranks positions g * 8 to (g + 1) * 8 - 1. The requests cached on one group are dealt out to the ranking groups in turn, so every pair of groups carries 8 // 4 or 2 requests and some pair carries exactly 2; the uneven part of the load is the live history lengths.
All inputs are finite; a program needn't handle non-finite values.
Results may differ from the reference program's by a relative error of at most 0.011.
Values may be sent and summed in bfloat16 or wider, within the bound.
A program may use at most 320 MiB of HBM per device.

```python
import math
import jax
import jax.numpy as jnp
import numpy as np
from jax import lax

D = 1024
HEADS = 8
HEAD_DIM = 128
BLK = 128
HIST_BLOCKS = 16
HIST_EV = 2048
CANDS = 512
REQ_GRP = 8
REQUESTS = 32


def assignment(key):
    key = jax.random.fold_in(key, 7)
    key_one, key_two, key_three, key_four = jax.random.split(key, 4)
    groups = REQUESTS // REQ_GRP
    request_perm = jax.random.permutation(key_one, REQUESTS).astype(jnp.int32)
    group_perm = jax.random.permutation(key_two, groups).astype(jnp.int32)
    local_scores = jax.random.randint(key_three, (groups, REQ_GRP), 0, 4096) * REQ_GRP + jnp.arange(REQ_GRP)[None, :]
    local_rank = jnp.argsort(jnp.argsort(local_scores, axis=1), axis=1).astype(jnp.int32)
    slot_ids = jnp.arange(REQUESTS, dtype=jnp.int32)
    owner_grp = slot_ids // REQ_GRP
    ranker = group_perm[(owner_grp + local_rank.reshape(-1)) % groups]
    tie_break = jax.random.randint(key_four, (REQUESTS,), 0, 4096) * REQUESTS + slot_ids
    rank_slot = jnp.argsort(ranker * (4096 * REQUESTS) + tie_break)
    return (request_perm, request_perm[rank_slot].astype(jnp.int32))


def draw_cache_request(key, part):
    return assignment(key)[0]


def draw_rank_request(key, part):
    return assignment(key)[1]


def levels(stream_key, dims, cuts, smallest, largest):
    level = 1.0
    for axis_at, parts in cuts:
        heights = jax.random.uniform(jax.random.fold_in(jax.random.fold_in(stream_key, 6), axis_at), (parts,), jnp.float32, smallest / len(cuts), largest / len(cuts))
        level = level * jnp.repeat(jnp.exp(heights), dims[axis_at] // parts).reshape((-1,) + (1,) * (len(dims) - 1 - axis_at))
    return level


def split_up(number_of, total, bound, skew):
    loads = [(1 << 20) // math.isqrt(grade ** skew) + 1 for grade in range(2, number_of + 1)]
    spare, holding = total - bound - (number_of - 1), [1] * (number_of - 1)
    while spare > 0:
        free = [i for i in range(number_of - 1) if holding[i] < bound]
        whole, budget = sum([loads[i] for i in free]), spare
        for i in free:
            extra = min(bound - holding[i], max(1, budget * loads[i] // whole), spare)
            holding[i] = holding[i] + extra
            spare = spare - extra
    return np.array([bound] + holding)


def uneven_parts(rng, number_of, total, reach, skew):
    if number_of == 2:
        one = jax.random.randint(rng, (), max(1, total - reach), min(reach, total - 1) + 1)
        return jnp.stack([one, total - one])
    tallies = jnp.asarray(split_up(number_of, total, reach, skew), jnp.int32)
    pairs = (number_of - 1) // 2
    giver, taker = tallies[1:1 + 2 * pairs:2], tallies[2:2 + 2 * pairs:2]
    room = jnp.minimum(giver - 1, reach - taker)
    passed = jax.random.randint(jax.random.fold_in(rng, 1), (pairs,), 0, 1 << 20) % (room + 1)
    tallies = tallies.at[1:1 + 2 * pairs:2].set(giver - passed).at[2:2 + 2 * pairs:2].set(taker + passed)
    return tallies[jax.random.permutation(jax.random.fold_in(rng, 2), number_of)]


def gaussian(stream_key, extent, deviation, bound, cuts=(), kind=jnp.bfloat16):
    entries = deviation * jax.random.normal(stream_key, extent, jnp.float32)
    if cuts:
        entries = entries * levels(stream_key, extent, cuts, -0.22, 0.18)
    return jnp.clip(entries, -bound, bound).astype(kind)


def setup_inputs(seed: int = 0) -> dict:
    splits = jax.random.split(jax.random.key(seed), 8)
    candidates = gaussian(splits[0], (CANDS, REQUESTS, D), 1.0, 6.0, ((0, 8), (1, 4)))
    kv_cache = gaussian(splits[1], (REQUESTS, HIST_EV, 2 * D), 1.0, 6.0, ((0, 4), (1, 8)))
    cache_request = draw_cache_request(jax.random.fold_in(splits[7], 71), 0)
    rank_request = draw_rank_request(jax.random.fold_in(splits[7], 71), 0)
    hist_blocks = uneven_parts(splits[4], REQUESTS, REQUESTS * (HIST_BLOCKS + 1) // 2, HIST_BLOCKS, 2).astype(jnp.int32)
    w_uq = gaussian(splits[5], (D, 2 * D), D ** -0.5, 0.1875)
    w_out = gaussian(splits[6], (D, D), D ** -0.5, 0.1875)
    return dict(candidates=candidates, kv_cache=kv_cache, cache_request=cache_request, rank_request=rank_request, hist_blocks=hist_blocks, w_uq=w_uq, w_out=w_out)


def layer_norm(values):
    center = values - lax.optimization_barrier(jnp.mean(values, axis=-1, keepdims=True))
    spread = lax.optimization_barrier(jnp.mean(center * center, axis=-1, keepdims=True))
    return center * lax.rsqrt(spread + 1e-05)

def reference(candidates, kv_cache, cache_request, rank_request, hist_blocks, w_uq, w_out):
    slot_ids = jnp.arange(REQUESTS, dtype=jnp.int32)
    match = cache_request[:, None] == rank_request[None, :]
    slot_of_pos = lax.optimization_barrier(jnp.sum(jnp.where(match, slot_ids[:, None], 0), axis=0)).astype(jnp.int32)
    live = (hist_blocks[rank_request] * BLK).astype(jnp.float32)
    inputs = candidates.astype(jnp.float32)
    normed = layer_norm(inputs).astype(jnp.bfloat16).reshape(CANDS * REQUESTS, D)
    projected = jax.nn.silu(jnp.dot(normed, w_uq, preferred_element_type=jnp.float32))
    gates = projected[:, :D].reshape(CANDS, REQUESTS, D)
    queries = projected[:, D:].astype(jnp.bfloat16).reshape(CANDS, REQUESTS, HEADS, HEAD_DIM)
    scale = HEAD_DIM ** (-0.5)
    events = jnp.arange(HIST_EV).astype(jnp.float32)

    def one_request(position):
        panel = kv_cache[slot_of_pos[position]].astype(jnp.float32)
        keys = panel[:, :D].reshape(HIST_EV, HEADS, HEAD_DIM)
        values = panel[:, D:].reshape(HIST_EV, HEADS, HEAD_DIM)
        query = lax.dynamic_index_in_dim(queries, position, 1, keepdims=False).astype(jnp.float32)
        scores = jnp.einsum('chd,ehd->hce', query, keys)
        keep = (events < live[position]).astype(jnp.float32) / live[position]
        weights = (jax.nn.silu(scores * scale) * keep).astype(jnp.bfloat16)
        return jnp.einsum('hce,ehd->chd', weights.astype(jnp.float32), values)
    mixed = lax.map(one_request, slot_ids)
    attn = jnp.moveaxis(mixed, 0, 1).reshape(CANDS, REQUESTS, D)
    gated = (layer_norm(attn) * gates).astype(jnp.bfloat16).reshape(CANDS * REQUESTS, D)
    result = jnp.dot(gated, w_out, preferred_element_type=jnp.float32) + inputs.reshape(CANDS * REQUESTS, D)
    return result.astype(jnp.bfloat16).reshape(CANDS, REQUESTS, D)
```

```python
import jax
import jax.numpy as jnp
from jax import lax
from jax.sharding import PartitionSpec as P

HEADS = 8
BLK = 128


def layer_norm(values):
    center = values - jnp.mean(values, axis=-1, keepdims=True)
    spread = jnp.mean(center * center, axis=-1, keepdims=True)
    return center * lax.rsqrt(spread + 1e-05)


def routing(cache_request, rank_request, per_group):
    slot_ids = jnp.arange(cache_request.shape[0], dtype=jnp.int32)
    match = cache_request[:, None] == rank_request[None, :]
    rank_pos = jnp.sum(jnp.where(match, slot_ids[None, :], 0), axis=1)
    target = rank_pos // per_group
    owner_grp = slot_ids // per_group
    earlier = (
        (owner_grp[:, None] == owner_grp[None, :])
        & (target[:, None] == target[None, :])
        & (slot_ids[None, :] < slot_ids[:, None])
    )
    arrival = jnp.sum(earlier.astype(jnp.int32), axis=1)
    slot_of_pos = jnp.sum(jnp.where(match, slot_ids[:, None], 0), axis=0)
    return (target, arrival, slot_of_pos)


def inverse(order):
    ids = jnp.arange(order.shape[0], dtype=jnp.int32)
    return jnp.sum(jnp.where(order[None, :] == ids[:, None], ids[None, :], 0), axis=1)


def on_device(candidates, kv_cache, cache_request, rank_request, hist_blocks, w_uq, w_out):
    groups = lax.axis_size("group")
    per_group, count, _ = kv_cache.shape
    cand_rows = candidates.shape[0]
    width = candidates.shape[2]
    head_dim = width // HEADS
    cap = per_group // groups
    group_now = lax.axis_index("group")
    member_now = lax.axis_index("member")
    target, arrival, slot_of_pos = routing(cache_request, rank_request, per_group)
    first = group_now * per_group
    local = first + jnp.arange(per_group, dtype=jnp.int32)
    source = slot_of_pos[local]
    unit_of_pos = source // per_group * cap + arrival[source]
    pos_of_unit = inverse(unit_of_pos)
    unit_of_slot = target[local] * cap + arrival[local]
    slot_of_unit = inverse(unit_of_slot)
    live = hist_blocks[cache_request[local]] * BLK

    inputs = candidates.astype(jnp.float32)
    normed = layer_norm(inputs).astype(jnp.bfloat16).reshape(cand_rows * per_group, width)
    projected = jax.nn.silu(jnp.dot(normed, w_uq, preferred_element_type=jnp.float32))
    gates = projected[:, :width].reshape(cand_rows, per_group, width)
    queries = projected[:, width:].astype(jnp.bfloat16).reshape(cand_rows, per_group, width)
    outgoing = jnp.transpose(queries, (1, 0, 2))[pos_of_unit]
    incoming = lax.all_to_all(outgoing, "group", split_axis=0, concat_axis=0, tiled=True)
    incoming = incoming[unit_of_slot]
    every = lax.all_gather(incoming, "member", axis=1, tiled=True)
    every = every.reshape(per_group, every.shape[1], HEADS, head_dim)
    keys = kv_cache[:, :, :width].reshape(per_group, count, HEADS, head_dim)
    values = kv_cache[:, :, width:].reshape(per_group, count, HEADS, head_dim)
    half = jnp.einsum("rchd,rehd->rhce", every, keys, preferred_element_type=jnp.float32) * (
        0.5 * head_dim**-0.5
    )
    events = member_now * count + jnp.arange(count)
    keep = (events[None, :] < live[:, None]).astype(jnp.float32) / live[:, None]
    weights = ((half + half * jnp.tanh(half)) * keep[:, None, None, :]).astype(jnp.bfloat16)
    partial = jnp.einsum("rhce,rehd->rchd", weights, values, preferred_element_type=jnp.float32)
    partial = partial.astype(jnp.bfloat16).reshape(per_group, every.shape[1], width)
    summed = lax.psum_scatter(partial, "member", scatter_dimension=1, tiled=True)
    back = lax.all_to_all(summed[slot_of_unit], "group", split_axis=0, concat_axis=0, tiled=True)
    attn = jnp.transpose(back[unit_of_pos], (1, 0, 2)).astype(jnp.float32)
    gated = (layer_norm(attn) * gates).astype(jnp.bfloat16).reshape(cand_rows * per_group, width)
    result = jnp.dot(gated, w_out, preferred_element_type=jnp.float32) + inputs.reshape(
        cand_rows * per_group, width
    )
    return result.astype(jnp.bfloat16).reshape(cand_rows, per_group, width)


def solution(mesh):
    return jax.shard_map(
        on_device,
        mesh=mesh,
        in_specs=(P("member", "group", None), P("group", "member", None), P(), P(), P(), P(), P()),
        out_specs=P("member", "group", None),
        check_vma=False,
    )
```

```python
import functools

import jax
import jax.numpy as jnp
from jax import lax
from jax.experimental import pallas as pl
from jax.experimental.pallas import tpu as pltpu
from jax.sharding import PartitionSpec as P

HEADS = 8
BLK = 128
LINE = 4


def layer_norm(values):
    center = values - jnp.mean(values, axis=-1, keepdims=True)
    spread = jnp.mean(center * center, axis=-1, keepdims=True)
    return center * lax.rsqrt(spread + 1e-05)


def routing(cache_request, rank_request, per_group):
    slot_ids = jnp.arange(cache_request.shape[0], dtype=jnp.int32)
    match = cache_request[:, None] == rank_request[None, :]
    rank_pos = jnp.sum(jnp.where(match, slot_ids[None, :], 0), axis=1)
    target = rank_pos // per_group
    owner_grp = slot_ids // per_group
    earlier = (
        (owner_grp[:, None] == owner_grp[None, :])
        & (target[:, None] == target[None, :])
        & (slot_ids[None, :] < slot_ids[:, None])
    )
    arrival = jnp.sum(earlier.astype(jnp.int32), axis=1)
    slot_of_pos = jnp.sum(jnp.where(match, slot_ids[:, None], 0), axis=0)
    return (target, arrival, slot_of_pos)


def inverse(order):
    ids = jnp.arange(order.shape[0], dtype=jnp.int32)
    return jnp.sum(jnp.where(order[None, :] == ids[:, None], ids[None, :], 0), axis=1)


def kernel(
    dims,
    slot_ref,
    live_ref,
    share_ref,
    q_ref,
    kv_hbm,
    out_ref,
    kv,
    qbuf,
    pbuf,
    prec,
    ssum,
    fin,
    kv_sem,
    s1,
    r1,
    s2,
    r2,
    s3,
    r3,
    s4,
    r4,
):
    groups, lines, rows, cap = dims
    units = groups * cap
    cands, width = q_ref.shape[1:]
    count = kv_hbm.shape[1]
    head_dim = width // HEADS
    g = lax.axis_index("group")
    member = lax.axis_index("member")
    z = member // rows
    x = lax.rem(member, rows)

    def at(group, line, row):
        return {"group": group, "member": line * rows + row}

    def add(value, step, size):
        return lax.rem(value + step, size)

    panel = pltpu.make_async_copy(kv_hbm, kv, kv_sem)
    panel.start()
    barrier = pltpu.get_barrier_semaphore()
    peers = [(t, dz, 0) for t in range(groups) for dz in range(lines) if t or dz]
    peers += [(0, 0, dx) for dx in range(1, rows)]
    for t, dz, dx in peers:
        pl.semaphore_signal(
            barrier,
            inc=1,
            device_id=at(add(g, t, groups), add(z, dz, lines), add(x, dx, rows)),
            device_id_type=pl.DeviceIdType.MESH,
        )
    pl.semaphore_wait(barrier, len(peers))

    def ready(ref, sem):
        pltpu.make_async_copy(ref, ref, sem).wait()

    def remote(src, dst, send, recv, device):
        return pltpu.make_async_remote_copy(
            src_ref=src,
            dst_ref=dst,
            send_sem=send,
            recv_sem=recv,
            device_id=device,
            device_id_type=pl.DeviceIdType.MESH,
        )

    def scatter_queries(u, carry):
        t = u // cap
        for dz in range(lines):
            there = (add(g, t, groups), add(z, dz, lines), x)
            send = lambda: remote(
                q_ref.at[u], qbuf.at[u, x, z], s1.at[u, dz], r1.at[u, dz], at(*there)
            ).start()
            if dz:
                send()
            else:
                pl.when(t > 0)(send)
                pl.when(t == 0)(
                    lambda: pltpu.make_async_copy(
                        q_ref.at[u], qbuf.at[u, x, z], r1.at[u, 0]
                    ).start()
                )
        return carry

    lax.fori_loop(0, units, scatter_queries, 0)
    panel.wait()

    def forward(u):
        for dz in range(lines):
            ready(qbuf.at[u, x, add(z, lines - dz, lines)], r1.at[u, dz])
        for dx in range(1, rows):
            remote(
                qbuf.at[u, x],
                qbuf.at[u, x],
                s2.at[u, dx],
                r2.at[u, dx],
                at(g, z, add(x, dx, rows)),
            ).start()

    def attend(u):
        for dx in range(1, rows):
            ready(qbuf.at[u, add(x, rows - dx, rows)], r2.at[u, dx])
        slot = slot_ref[u]
        limit = live_ref[u] - member * count
        share = share_ref[u]
        keep = lax.broadcasted_iota(jnp.int32, (count, head_dim), 0) < limit
        keep = keep.astype(jnp.float32)
        for h in range(HEADS):
            cols = slice(h * head_dim, (h + 1) * head_dim)
            vals = slice(width + h * head_dim, width + (h + 1) * head_dim)
            q = qbuf[u, :, :, :, cols].reshape(rows * lines * cands, head_dim)
            k = kv[slot, :, cols]
            v = (kv[slot, :, vals].astype(jnp.float32) * keep).astype(jnp.bfloat16)
            score = lax.dot_general(
                q, k, (((1,), (1,)), ((), ())), preferred_element_type=jnp.float32
            )
            half = score * (0.5 * head_dim**-0.5)
            weight = (half + half * jnp.tanh(half)).astype(jnp.bfloat16)
            part = jnp.dot(weight, v, preferred_element_type=jnp.float32) * share
            pbuf[u, :, :, :, cols] = part.astype(jnp.bfloat16).reshape(
                rows, lines, cands, head_dim
            )
        for dx in range(1, rows):
            row = add(x, dx, rows)
            remote(
                pbuf.at[u, row], prec.at[u, dx], s3.at[u, dx], r3.at[u, dx], at(g, z, row)
            ).start()

    def give_back(u):
        t = u // cap
        for dx in range(1, rows):
            ready(prec.at[u, dx], r3.at[u, dx])
        total = pbuf[u, x].astype(jnp.float32)
        for dx in range(1, rows):
            total = total + prec[u, dx].astype(jnp.float32)
        ssum[u] = total.astype(jnp.bfloat16)
        for dz in range(lines):
            line = add(z, dz, lines)
            there = (add(g, groups - t, groups), line, x)
            send = lambda: remote(
                ssum.at[u, line], fin.at[u, dz], s4.at[u, dz], r4.at[u, dz], at(*there)
            ).start()
            if dz:
                send()
            else:
                pl.when(t > 0)(send)
                pl.when(t == 0)(
                    lambda: pltpu.make_async_copy(
                        ssum.at[u, line], fin.at[u, 0], r4.at[u, 0]
                    ).start()
                )

    def stage(i, carry):
        pl.when(i < units)(lambda: forward(i))
        pl.when((i >= 1) & (i < units + 1))(lambda: attend(i - 1))
        pl.when(i >= 2)(lambda: give_back(i - 2))
        return carry

    lax.fori_loop(0, units + 2, stage, 0)

    def collect(u, carry):
        for dz in range(lines):
            ready(fin.at[u, dz], r4.at[u, dz])
        total = fin[u, 0].astype(jnp.float32)
        for dz in range(1, lines):
            total = total + fin[u, dz].astype(jnp.float32)
        out_ref[u] = total
        return carry

    lax.fori_loop(0, units, collect, 0)

    def drain(u, carry):
        t = u // cap
        for dz in range(lines):
            def both():
                ready(q_ref.at[u], s1.at[u, dz])
                ready(ssum.at[u, add(z, dz, lines)], s4.at[u, dz])

            if dz:
                both()
            else:
                pl.when(t > 0)(both)
        for dx in range(1, rows):
            ready(qbuf.at[u, x], s2.at[u, dx])
            ready(pbuf.at[u, add(x, dx, rows)], s3.at[u, dx])
        return carry

    lax.fori_loop(0, units, drain, 0)


def exchange(outgoing, kv_cache, slot_of_unit, live, groups, members):
    units, cands, width = outgoing.shape
    lines = LINE
    rows = members // lines
    cap = units // groups
    count = kv_cache.shape[1]
    smem = pl.BlockSpec(memory_space=pltpu.SMEM)
    vmem = pl.BlockSpec(memory_space=pltpu.VMEM)
    sixteen = jnp.bfloat16
    sem = pltpu.SemaphoreType.DMA
    return pl.pallas_call(
        functools.partial(kernel, (groups, lines, rows, cap)),
        out_shape=jax.ShapeDtypeStruct(outgoing.shape, jnp.float32),
        in_specs=[smem, smem, smem, vmem, pl.BlockSpec(memory_space=pl.ANY)],
        out_specs=vmem,
        scratch_shapes=[
            pltpu.VMEM(kv_cache.shape, sixteen),
            pltpu.VMEM((units, rows, lines, cands, width), sixteen),
            pltpu.VMEM((units, rows, lines, cands, width), sixteen),
            pltpu.VMEM((units, rows, lines, cands, width), sixteen),
            pltpu.VMEM((units, lines, cands, width), sixteen),
            pltpu.VMEM((units, lines, cands, width), sixteen),
            sem,
            sem((units, lines)),
            sem((units, lines)),
            sem((units, rows)),
            sem((units, rows)),
            sem((units, rows)),
            sem((units, rows)),
            sem((units, lines)),
            sem((units, lines)),
        ],
        compiler_params=pltpu.CompilerParams(
            collective_id=0, has_side_effects=True, vmem_limit_bytes=56 * 1024 * 1024
        ),
        cost_estimate=pl.CostEstimate(
            flops=4 * units * cands * members * count * width,
            bytes_accessed=2 * kv_cache.size,
            transcendentals=units * cands * members * count * HEADS,
        ),
    )(slot_of_unit, live, 1.0 / live.astype(jnp.float32), outgoing, kv_cache)


def on_device(candidates, kv_cache, cache_request, rank_request, hist_blocks, w_uq, w_out):
    groups = lax.axis_size("group")
    per_group, count, _ = kv_cache.shape
    cand_rows = candidates.shape[0]
    width = candidates.shape[2]
    head_dim = width // HEADS
    cap = per_group // groups
    group_now = lax.axis_index("group")
    members = lax.axis_size("member")
    target, arrival, slot_of_pos = routing(cache_request, rank_request, per_group)
    first = group_now * per_group
    local = first + jnp.arange(per_group, dtype=jnp.int32)
    source = slot_of_pos[local]
    hops = lax.rem(source // per_group - group_now + groups, groups)
    unit_of_pos = hops * cap + arrival[source]
    pos_of_unit = inverse(unit_of_pos)
    unit_of_slot = lax.rem(group_now - target[local] + groups, groups) * cap + arrival[local]
    slot_of_unit = inverse(unit_of_slot)
    live = hist_blocks[cache_request[local]][slot_of_unit] * BLK

    inputs = candidates.astype(jnp.float32)
    normed = layer_norm(inputs).astype(jnp.bfloat16).reshape(cand_rows * per_group, width)
    projected = jax.nn.silu(jnp.dot(normed, w_uq, preferred_element_type=jnp.float32))
    gates = projected[:, :width].reshape(cand_rows, per_group, width)
    queries = projected[:, width:].astype(jnp.bfloat16).reshape(cand_rows, per_group, width)
    outgoing = jnp.transpose(queries, (1, 0, 2))[pos_of_unit]
    sums = exchange(outgoing, kv_cache, slot_of_unit, live, groups, members)
    attn = jnp.transpose(sums[unit_of_pos], (1, 0, 2))
    gated = (layer_norm(attn) * gates).astype(jnp.bfloat16).reshape(cand_rows * per_group, width)
    result = jnp.dot(gated, w_out, preferred_element_type=jnp.float32) + inputs.reshape(
        cand_rows * per_group, width
    )
    return result.astype(jnp.bfloat16).reshape(cand_rows, per_group, width)


def solution(mesh):
    return jax.shard_map(
        on_device,
        mesh=mesh,
        in_specs=(P("member", "group", None), P("group", "member", None), P(), P(), P(), P(), P()),
        out_specs=P("member", "group", None),
        check_vma=False,
    )
```

```python
import functools

import jax
import jax.numpy as jnp
from jax import lax
from jax.experimental import pallas as pl
from jax.experimental.pallas import tpu as pltpu
from jax.sharding import PartitionSpec as P

HEADS = 8
BLK = 128
LINE = 4


def layer_norm(values):
    center = values - jnp.mean(values, axis=-1, keepdims=True)
    spread = jnp.mean(center * center, axis=-1, keepdims=True)
    return center * lax.rsqrt(spread + 1e-05)


def routing(cache_request, rank_request, hist_blocks, per_group, groups, group_now):
    cap = per_group // groups
    first = group_now * per_group
    slot_ids = jnp.arange(cache_request.shape[0], dtype=jnp.int32)
    match = cache_request[:, None] == rank_request[None, :]
    rank_pos = jnp.sum(jnp.where(match, slot_ids[None, :], 0), axis=1)
    target = rank_pos // per_group
    owner_grp = slot_ids // per_group
    earlier = (
        (owner_grp[:, None] == owner_grp[None, :])
        & (target[:, None] == target[None, :])
        & (slot_ids[None, :] < slot_ids[:, None])
    )
    arrival = jnp.sum(earlier.astype(jnp.int32), axis=1)
    leaving = lax.rem(owner_grp - group_now + groups, groups) * cap + arrival
    arriving = lax.rem(group_now - target + groups, groups) * cap + arrival
    ids = jnp.arange(per_group, dtype=jnp.int32)
    ranked_here = lax.dynamic_slice_in_dim(rank_request, first, per_group)
    unit_of_pos = jnp.sum(
        jnp.where(cache_request[:, None] == ranked_here[None, :], leaving[:, None], 0), axis=0
    )
    mine = owner_grp == group_now
    slot_of_unit = jnp.sum(
        jnp.where(
            mine[:, None] & (arriving[:, None] == ids[None, :]), (slot_ids - first)[:, None], 0
        ),
        axis=0,
    )
    cached_here = lax.dynamic_slice_in_dim(cache_request, first, per_group)
    blocks = jnp.sum(
        jnp.where(slot_ids[:, None] == cached_here[None, :], hist_blocks[:, None], 0), axis=0
    )
    return unit_of_pos, inverse(unit_of_pos), slot_of_unit, blocks * BLK


def inverse(order):
    ids = jnp.arange(order.shape[0], dtype=jnp.int32)
    return jnp.sum(jnp.where(order[None, :] == ids[:, None], ids[None, :], 0), axis=1)


def kernel(
    dims,
    pos_ref,
    unit_ref,
    slot_ref,
    live_ref,
    share_ref,
    q_ref,
    kv_hbm,
    out_ref,
    qown,
    kv,
    qbuf,
    pbuf,
    prec,
    ssum,
    fin,
    kv_sem,
    s1,
    r1,
    s2,
    r2,
    s3,
    r3,
    s4,
    r4,
):
    groups, lines, rows, cap = dims
    units = groups * cap
    cands, width = q_ref.shape[1:]
    count = kv_hbm.shape[1]
    head_dim = width // HEADS
    g = lax.axis_index("group")
    member = lax.axis_index("member")
    z = member // rows
    x = lax.rem(member, rows)

    def at(group, line, row):
        return {"group": group, "member": line * rows + row}

    def add(value, step, size):
        return lax.rem(value + step, size)

    panel = pltpu.make_async_copy(kv_hbm, kv, kv_sem)
    panel.start()
    barrier = pltpu.get_barrier_semaphore()
    peers = [(t, dz, 0) for t in range(groups) for dz in range(lines) if t or dz]
    peers += [(0, 0, dx) for dx in range(1, rows)]
    for t, dz, dx in peers:
        pl.semaphore_signal(
            barrier,
            inc=1,
            device_id=at(add(g, t, groups), add(z, dz, lines), add(x, dx, rows)),
            device_id_type=pl.DeviceIdType.MESH,
        )
    pl.semaphore_wait(barrier, len(peers))

    def ready(ref, sem):
        pltpu.make_async_copy(ref, ref, sem).wait()

    def remote(src, dst, send, recv, device):
        return pltpu.make_async_remote_copy(
            src_ref=src,
            dst_ref=dst,
            send_sem=send,
            recv_sem=recv,
            device_id=device,
            device_id_type=pl.DeviceIdType.MESH,
        )

    def scatter_queries(u, carry):
        t = u // cap
        qown[u] = q_ref[pos_ref[u]]
        for dz in range(lines):
            there = (add(g, t, groups), add(z, dz, lines), x)
            send = lambda: remote(
                qown.at[u], qbuf.at[u, x, z], s1.at[u, dz], r1.at[u, dz], at(*there)
            ).start()
            if dz:
                send()
            else:
                pl.when(t > 0)(send)
                pl.when(t == 0)(
                    lambda: pltpu.make_async_copy(
                        qown.at[u], qbuf.at[u, x, z], r1.at[u, 0]
                    ).start()
                )
        return carry

    lax.fori_loop(0, units, scatter_queries, 0)

    def forward(u):
        for dz in range(lines):
            line = add(z, lines - dz, lines)
            ready(qbuf.at[u, x, line], r1.at[u, dz])
            for dx in range(1, rows):
                remote(
                    qbuf.at[u, x, line],
                    qbuf.at[u, x, line],
                    s2.at[u, dx, dz],
                    r2.at[u, dx, dz],
                    at(g, z, add(x, dx, rows)),
                ).start()

    def attend(u):
        for dx in range(1, rows):
            for dz in range(lines):
                line = add(z, lines - dz, lines)
                ready(qbuf.at[u, add(x, rows - dx, rows), line], r2.at[u, dx, dz])
        slot = slot_ref[u]
        limit = live_ref[slot] - member * count
        share = share_ref[slot]
        keep = lax.broadcasted_iota(jnp.int32, (count, head_dim), 0) < limit
        keep = keep.astype(jnp.float32)
        for h in range(HEADS):
            cols = slice(h * head_dim, (h + 1) * head_dim)
            vals = slice(width + h * head_dim, width + (h + 1) * head_dim)
            q = qbuf[u, :, :, :, cols].reshape(rows * lines * cands, head_dim)
            k = kv[slot, :, cols]
            v = (kv[slot, :, vals].astype(jnp.float32) * keep).astype(jnp.bfloat16)
            score = lax.dot_general(
                q, k, (((1,), (1,)), ((), ())), preferred_element_type=jnp.float32
            )
            half = score * (0.5 * head_dim**-0.5)
            weight = (half + half * jnp.tanh(half)).astype(jnp.bfloat16)
            part = jnp.dot(weight, v, preferred_element_type=jnp.float32) * share
            pbuf[u, :, :, :, cols] = part.astype(jnp.bfloat16).reshape(
                rows, lines, cands, head_dim
            )
        for dx in range(1, rows):
            row = add(x, dx, rows)
            remote(
                pbuf.at[u, row], prec.at[u, dx], s3.at[u, dx], r3.at[u, dx], at(g, z, row)
            ).start()

    def give_back(u):
        t = u // cap
        for dx in range(1, rows):
            ready(prec.at[u, dx], r3.at[u, dx])
        total = pbuf[u, x].astype(jnp.float32)
        for dx in range(1, rows):
            total = total + prec[u, dx].astype(jnp.float32)
        ssum[u] = total.astype(jnp.bfloat16)
        for dz in range(lines):
            line = add(z, dz, lines)
            there = (add(g, groups - t, groups), line, x)
            send = lambda: remote(
                ssum.at[u, line], fin.at[u, dz], s4.at[u, dz], r4.at[u, dz], at(*there)
            ).start()
            if dz:
                send()
            else:
                pl.when(t > 0)(send)
                pl.when(t == 0)(
                    lambda: pltpu.make_async_copy(
                        ssum.at[u, line], fin.at[u, 0], r4.at[u, 0]
                    ).start()
                )

    def stage(i, carry):
        pl.when(i < units)(lambda: forward(i))
        pl.when(i == 1)(panel.wait)
        pl.when((i >= 1) & (i < units + 1))(lambda: attend(i - 1))
        pl.when(i >= 2)(lambda: give_back(i - 2))
        return carry

    lax.fori_loop(0, units + 2, stage, 0)

    def arrived(u, carry):
        for dz in range(lines):
            ready(fin.at[u, dz], r4.at[u, dz])
        return carry

    lax.fori_loop(0, units, arrived, 0)

    def collect(p, carry):
        u = unit_ref[p]
        total = fin[u, 0].astype(jnp.float32)
        for dz in range(1, lines):
            total = total + fin[u, dz].astype(jnp.float32)
        out_ref[p] = total
        return carry

    lax.fori_loop(0, units, collect, 0)

    def drain(u, carry):
        t = u // cap
        for dz in range(lines):
            def both():
                ready(qown.at[u], s1.at[u, dz])
                ready(ssum.at[u, add(z, dz, lines)], s4.at[u, dz])

            if dz:
                both()
            else:
                pl.when(t > 0)(both)
        for dx in range(1, rows):
            for dz in range(lines):
                ready(qbuf.at[u, x, add(z, lines - dz, lines)], s2.at[u, dx, dz])
            ready(pbuf.at[u, add(x, dx, rows)], s3.at[u, dx])
        return carry

    lax.fori_loop(0, units, drain, 0)


def exchange(routes, queries, kv_cache, groups, members):
    units, cands, width = queries.shape
    lines = LINE
    rows = members // lines
    cap = units // groups
    count = kv_cache.shape[1]
    smem = pl.BlockSpec(memory_space=pltpu.SMEM)
    vmem = pl.BlockSpec(memory_space=pltpu.VMEM)
    sixteen = jnp.bfloat16
    sem = pltpu.SemaphoreType.DMA
    return pl.pallas_call(
        functools.partial(kernel, (groups, lines, rows, cap)),
        out_shape=jax.ShapeDtypeStruct(queries.shape, jnp.float32),
        in_specs=[smem] * 5 + [vmem, pl.BlockSpec(memory_space=pl.ANY)],
        out_specs=vmem,
        scratch_shapes=[
            pltpu.VMEM(queries.shape, sixteen),
            pltpu.VMEM(kv_cache.shape, sixteen),
            pltpu.VMEM((units, rows, lines, cands, width), sixteen),
            pltpu.VMEM((units, rows, lines, cands, width), sixteen),
            pltpu.VMEM((units, rows, lines, cands, width), sixteen),
            pltpu.VMEM((units, lines, cands, width), sixteen),
            pltpu.VMEM((units, lines, cands, width), sixteen),
            sem,
            sem((units, lines)),
            sem((units, lines)),
            sem((units, rows, lines)),
            sem((units, rows, lines)),
            sem((units, rows)),
            sem((units, rows)),
            sem((units, lines)),
            sem((units, lines)),
        ],
        compiler_params=pltpu.CompilerParams(
            collective_id=0, has_side_effects=True, vmem_limit_bytes=56 * 1024 * 1024
        ),
        cost_estimate=pl.CostEstimate(
            flops=4 * units * cands * members * count * width,
            bytes_accessed=2 * kv_cache.size,
            transcendentals=units * cands * members * count * HEADS,
        ),
    )(*routes, queries, kv_cache)


def on_device(candidates, kv_cache, cache_request, rank_request, hist_blocks, w_uq, w_out):
    groups = lax.axis_size("group")
    per_group = kv_cache.shape[0]
    cand_rows = candidates.shape[0]
    width = candidates.shape[2]
    group_now = lax.axis_index("group")
    members = lax.axis_size("member")
    unit_of_pos, pos_of_unit, slot_of_unit, live = routing(
        cache_request, rank_request, hist_blocks, per_group, groups, group_now
    )
    inputs = jnp.transpose(candidates, (1, 0, 2)).astype(jnp.float32)
    normed = layer_norm(inputs).astype(jnp.bfloat16).reshape(per_group * cand_rows, width)
    projected = jax.nn.silu(jnp.dot(normed, w_uq, preferred_element_type=jnp.float32))
    gates = projected[:, :width].reshape(per_group, cand_rows, width)
    queries = projected[:, width:].astype(jnp.bfloat16).reshape(per_group, cand_rows, width)
    routes = (pos_of_unit, unit_of_pos, slot_of_unit, live, 1.0 / live.astype(jnp.float32))
    attn = exchange(routes, queries, kv_cache, groups, members)
    gated = (layer_norm(attn) * gates).astype(jnp.bfloat16).reshape(cand_rows * per_group, width)
    result = jnp.dot(gated, w_out, preferred_element_type=jnp.float32) + inputs.reshape(
        cand_rows * per_group, width
    )
    result = result.astype(jnp.bfloat16).reshape(per_group, cand_rows, width)
    return jnp.transpose(result, (1, 0, 2))


def solution(mesh):
    return jax.shard_map(
        on_device,
        mesh=mesh,
        in_specs=(P("member", "group", None), P("group", "member", None), P(), P(), P(), P(), P()),
        out_specs=P("member", "group", None),
        check_vma=False,
    )
```

```python
import functools

import jax
import jax.numpy as jnp
from jax import lax
from jax.experimental import pallas as pl
from jax.experimental.pallas import tpu as pltpu
from jax.sharding import PartitionSpec as P

HEADS = 8
BLK = 128
LINE = 4
AHEAD = 2


def layer_norm(values):
    center = values - jnp.mean(values, axis=-1, keepdims=True)
    spread = jnp.mean(center * center, axis=-1, keepdims=True)
    return center * lax.rsqrt(spread + 1e-05)


def routing(cache_request, rank_request, per_group, groups, group_now):
    cap = per_group // groups
    first = group_now * per_group
    slot_ids = jnp.arange(cache_request.shape[0], dtype=jnp.int32)
    match = cache_request[:, None] == rank_request[None, :]
    rank_pos = jnp.sum(jnp.where(match, slot_ids[None, :], 0), axis=1)
    target = rank_pos // per_group
    owner_grp = slot_ids // per_group
    earlier = (
        (owner_grp[:, None] == owner_grp[None, :])
        & (target[:, None] == target[None, :])
        & (slot_ids[None, :] < slot_ids[:, None])
    )
    arrival = jnp.sum(earlier.astype(jnp.int32), axis=1)
    leaving = lax.rem(owner_grp - group_now + groups, groups) * cap + arrival
    arriving = lax.rem(group_now - target + groups, groups) * cap + arrival
    ids = jnp.arange(per_group, dtype=jnp.int32)
    unit_of_pos = jnp.sum(jnp.where(match, leaving[:, None], 0), axis=0)
    ranks = (target == group_now)[:, None] & (leaving[:, None] == ids[None, :])
    pos_of_unit = jnp.sum(jnp.where(ranks, (rank_pos - first)[:, None], 0), axis=0)
    holds = (owner_grp == group_now)[:, None] & (arriving[:, None] == ids[None, :])
    slot_of_unit = jnp.sum(jnp.where(holds, (slot_ids - first)[:, None], 0), axis=0)
    return pos_of_unit, unit_of_pos, slot_of_unit


def kernel(
    dims,
    pos_ref,
    unit_ref,
    slot_ref,
    cache_ref,
    blocks_ref,
    q_ref,
    kv_hbm,
    out_ref,
    qown,
    kv,
    qbuf,
    pbuf,
    prec,
    ssum,
    fin,
    kv_sem,
    s1,
    r1,
    s2,
    r2,
    s3,
    r3,
    s4,
    r4,
):
    groups, lines, rows, cap = dims
    units = groups * cap
    cands, width = q_ref.shape[1:]
    count = kv_hbm.shape[1]
    head_dim = width // HEADS
    g = lax.axis_index("group")
    member = lax.axis_index("member")
    z = member // rows
    x = lax.rem(member, rows)

    def at(group, line, row):
        return {"group": group, "member": line * rows + row}

    def add(value, step, size):
        return lax.rem(value + step, size)

    panel = pltpu.make_async_copy(kv_hbm, kv, kv_sem)
    panel.start()
    barrier = pltpu.get_barrier_semaphore()
    peers = [(t, dz, 0) for t in range(groups) for dz in range(lines) if t or dz]
    peers += [(0, 0, dx) for dx in range(1, rows)]
    for t, dz, dx in peers:
        pl.semaphore_signal(
            barrier,
            inc=1,
            device_id=at(add(g, t, groups), add(z, dz, lines), add(x, dx, rows)),
            device_id_type=pl.DeviceIdType.MESH,
        )
    pl.semaphore_wait(barrier, len(peers))

    def ready(ref, sem):
        pltpu.make_async_copy(ref, ref, sem).wait()

    def remote(src, dst, send, recv, device):
        return pltpu.make_async_remote_copy(
            src_ref=src,
            dst_ref=dst,
            send_sem=send,
            recv_sem=recv,
            device_id=device,
            device_id_type=pl.DeviceIdType.MESH,
        )

    def scatter_queries(u, carry=0):
        t = u // cap
        qown[u] = q_ref[pos_ref[u]]
        for dz in range(lines):
            there = (add(g, t, groups), add(z, dz, lines), x)
            send = lambda: remote(
                qown.at[u], qbuf.at[u, x, z], s1.at[u, dz], r1.at[u, dz], at(*there)
            ).start()
            if dz:
                send()
            else:
                pl.when(t > 0)(send)
                pl.when(t == 0)(
                    lambda: pltpu.make_async_copy(
                        qown.at[u], qbuf.at[u, x, z], r1.at[u, 0]
                    ).start()
                )
        return carry

    lax.fori_loop(0, min(AHEAD, units), scatter_queries, 0)

    def forward(u):
        for dz in range(lines):
            line = add(z, lines - dz, lines)
            ready(qbuf.at[u, x, line], r1.at[u, dz])
            for dx in range(1, rows):
                remote(
                    qbuf.at[u, x, line],
                    qbuf.at[u, x, line],
                    s2.at[u, dx, dz],
                    r2.at[u, dx, dz],
                    at(g, z, add(x, dx, rows)),
                ).start()

    def attend(u):
        for dx in range(1, rows):
            for dz in range(lines):
                line = add(z, lines - dz, lines)
                ready(qbuf.at[u, add(x, rows - dx, rows), line], r2.at[u, dx, dz])
        slot = slot_ref[u]
        live = blocks_ref[cache_ref[g * units + slot]] * BLK
        limit = live - member * count
        share = 1.0 / jnp.full((8, head_dim), live, jnp.int32).astype(jnp.float32)
        share = share[0:1, :]
        keep = lax.broadcasted_iota(jnp.int32, (count, head_dim), 0) < limit
        keep = keep.astype(jnp.float32)
        for h in range(HEADS):
            cols = slice(h * head_dim, (h + 1) * head_dim)
            vals = slice(width + h * head_dim, width + (h + 1) * head_dim)
            q = qbuf[u, :, :, :, cols].reshape(rows * lines * cands, head_dim)
            k = kv[slot, :, cols]
            v = (kv[slot, :, vals].astype(jnp.float32) * keep).astype(jnp.bfloat16)
            score = lax.dot_general(
                q, k, (((1,), (1,)), ((), ())), preferred_element_type=jnp.float32
            )
            half = score * (0.5 * head_dim**-0.5)
            weight = (half + half * jnp.tanh(half)).astype(jnp.bfloat16)
            part = jnp.dot(weight, v, preferred_element_type=jnp.float32) * share
            pbuf[u, :, :, :, cols] = part.astype(jnp.bfloat16).reshape(
                rows, lines, cands, head_dim
            )
        for dx in range(1, rows):
            row = add(x, dx, rows)
            remote(
                pbuf.at[u, row], prec.at[u, dx], s3.at[u, dx], r3.at[u, dx], at(g, z, row)
            ).start()

    def give_back(u):
        t = u // cap
        for dx in range(1, rows):
            ready(prec.at[u, dx], r3.at[u, dx])
        total = pbuf[u, x].astype(jnp.float32)
        for dx in range(1, rows):
            total = total + prec[u, dx].astype(jnp.float32)
        ssum[u] = total.astype(jnp.bfloat16)
        for dz in range(lines):
            line = add(z, dz, lines)
            there = (add(g, groups - t, groups), line, x)
            send = lambda: remote(
                ssum.at[u, line], fin.at[u, dz], s4.at[u, dz], r4.at[u, dz], at(*there)
            ).start()
            if dz:
                send()
            else:
                pl.when(t > 0)(send)
                pl.when(t == 0)(
                    lambda: pltpu.make_async_copy(
                        ssum.at[u, line], fin.at[u, 0], r4.at[u, 0]
                    ).start()
                )

    def later(u):
        scatter_queries(u)

    def stage(i, carry):
        pl.when(i < units)(lambda: forward(i))
        pl.when(i + AHEAD < units)(lambda: later(i + AHEAD))
        pl.when(i == 1)(panel.wait)
        pl.when((i >= 1) & (i < units + 1))(lambda: attend(i - 1))
        pl.when(i >= 2)(lambda: give_back(i - 2))
        return carry

    lax.fori_loop(0, units + 2, stage, 0)

    def arrived(u, carry):
        for dz in range(lines):
            ready(fin.at[u, dz], r4.at[u, dz])
        return carry

    lax.fori_loop(0, units, arrived, 0)

    def collect(p, carry):
        u = unit_ref[g * units + p]
        total = fin[u, 0].astype(jnp.float32)
        for dz in range(1, lines):
            total = total + fin[u, dz].astype(jnp.float32)
        out_ref[p] = layer_norm(total)
        return carry

    lax.fori_loop(0, units, collect, 0)

    def drain(u, carry):
        t = u // cap
        for dz in range(lines):
            def both():
                ready(qown.at[u], s1.at[u, dz])
                ready(ssum.at[u, add(z, dz, lines)], s4.at[u, dz])

            if dz:
                both()
            else:
                pl.when(t > 0)(both)
        for dx in range(1, rows):
            for dz in range(lines):
                ready(qbuf.at[u, x, add(z, lines - dz, lines)], s2.at[u, dx, dz])
            ready(pbuf.at[u, add(x, dx, rows)], s3.at[u, dx])
        return carry

    lax.fori_loop(0, units, drain, 0)


def exchange(routes, queries, kv_cache, groups, members):
    units, cands, width = queries.shape
    lines = LINE
    rows = members // lines
    cap = units // groups
    count = kv_cache.shape[1]
    smem = pl.BlockSpec(memory_space=pltpu.SMEM)
    vmem = pl.BlockSpec(memory_space=pltpu.VMEM)
    sixteen = jnp.bfloat16
    sem = pltpu.SemaphoreType.DMA
    return pl.pallas_call(
        functools.partial(kernel, (groups, lines, rows, cap)),
        out_shape=jax.ShapeDtypeStruct(queries.shape, jnp.float32),
        in_specs=[smem] * 5 + [vmem, pl.BlockSpec(memory_space=pl.ANY)],
        out_specs=vmem,
        scratch_shapes=[
            pltpu.VMEM(queries.shape, sixteen),
            pltpu.VMEM(kv_cache.shape, sixteen),
            pltpu.VMEM((units, rows, lines, cands, width), sixteen),
            pltpu.VMEM((units, rows, lines, cands, width), sixteen),
            pltpu.VMEM((units, rows, lines, cands, width), sixteen),
            pltpu.VMEM((units, lines, cands, width), sixteen),
            pltpu.VMEM((units, lines, cands, width), sixteen),
            sem,
            sem((units, lines)),
            sem((units, lines)),
            sem((units, rows, lines)),
            sem((units, rows, lines)),
            sem((units, rows)),
            sem((units, rows)),
            sem((units, lines)),
            sem((units, lines)),
        ],
        compiler_params=pltpu.CompilerParams(
            collective_id=0, has_side_effects=True, vmem_limit_bytes=56 * 1024 * 1024
        ),
        cost_estimate=pl.CostEstimate(
            flops=4 * units * cands * members * count * width,
            bytes_accessed=2 * kv_cache.size,
            transcendentals=units * cands * members * count * HEADS,
        ),
    )(*routes, queries, kv_cache)


def on_device(candidates, kv_cache, cache_request, rank_request, hist_blocks, w_uq, w_out):
    groups = lax.axis_size("group")
    per_group = kv_cache.shape[0]
    cand_rows = candidates.shape[0]
    width = candidates.shape[2]
    group_now = lax.axis_index("group")
    members = lax.axis_size("member")
    routes = routing(cache_request, rank_request, per_group, groups, group_now)
    routes += (cache_request, hist_blocks)
    inputs = jnp.transpose(candidates, (1, 0, 2)).astype(jnp.float32)
    normed = layer_norm(inputs).astype(jnp.bfloat16).reshape(per_group * cand_rows, width)
    projected = jax.nn.silu(jnp.dot(normed, w_uq, preferred_element_type=jnp.float32))
    gates = projected[:, :width].reshape(per_group, cand_rows, width)
    queries = projected[:, width:].astype(jnp.bfloat16).reshape(per_group, cand_rows, width)
    attn = exchange(routes, queries, kv_cache, groups, members)
    gated = (attn * gates).astype(jnp.bfloat16).reshape(cand_rows * per_group, width)
    result = jnp.dot(gated, w_out, preferred_element_type=jnp.float32) + inputs.reshape(
        cand_rows * per_group, width
    )
    result = result.astype(jnp.bfloat16).reshape(per_group, cand_rows, width)
    return jnp.transpose(result, (1, 0, 2))


def solution(mesh):
    return jax.shard_map(
        on_device,
        mesh=mesh,
        in_specs=(P("member", "group", None), P("group", "member", None), P(), P(), P(), P(), P()),
        out_specs=P("member", "group", None),
        check_vma=False,
    )
```

```python
import functools

import jax
import jax.numpy as jnp
from jax import lax
from jax.experimental import pallas as pl
from jax.experimental.pallas import tpu as pltpu
from jax.sharding import PartitionSpec as P

HEADS = 8
BLK = 128
LINE = 4
AHEAD = 2


def layer_norm(values):
    center = values - jnp.mean(values, axis=-1, keepdims=True)
    spread = jnp.mean(center * center, axis=-1, keepdims=True)
    return center * lax.rsqrt(spread + 1e-05)


def routing(cache_request, rank_request, per_group, groups, group_now):
    cap = per_group // groups
    first = group_now * per_group
    slot_ids = jnp.arange(cache_request.shape[0], dtype=jnp.int32)
    match = cache_request[:, None] == rank_request[None, :]
    rank_pos = jnp.sum(jnp.where(match, slot_ids[None, :], 0), axis=1)
    target = rank_pos // per_group
    owner_grp = slot_ids // per_group
    earlier = (
        (owner_grp[:, None] == owner_grp[None, :])
        & (target[:, None] == target[None, :])
        & (slot_ids[None, :] < slot_ids[:, None])
    )
    arrival = jnp.sum(earlier.astype(jnp.int32), axis=1)
    leaving = lax.rem(owner_grp - group_now + groups, groups) * cap + arrival
    arriving = lax.rem(group_now - target + groups, groups) * cap + arrival
    ids = jnp.arange(per_group, dtype=jnp.int32)
    unit_of_pos = jnp.sum(jnp.where(match, leaving[:, None], 0), axis=0)
    ranks = (target == group_now)[:, None] & (leaving[:, None] == ids[None, :])
    pos_of_unit = jnp.sum(jnp.where(ranks, (rank_pos - first)[:, None], 0), axis=0)
    holds = (owner_grp == group_now)[:, None] & (arriving[:, None] == ids[None, :])
    slot_of_unit = jnp.sum(jnp.where(holds, (slot_ids - first)[:, None], 0), axis=0)
    return pos_of_unit, unit_of_pos, slot_of_unit


def kernel(
    dims,
    pos_ref,
    unit_ref,
    slot_ref,
    cache_ref,
    blocks_ref,
    q_ref,
    kv_hbm,
    out_ref,
    qown,
    kv,
    qbuf,
    pbuf,
    prec,
    ssum,
    fin,
    kv_sem,
    s1,
    r1,
    s2,
    r2,
    s3,
    r3,
    s4,
    r4,
    s5,
    r5,
):
    groups, lines, rows, cap = dims
    units = groups * cap
    cands, width = q_ref.shape[1:]
    count = kv_hbm.shape[1]
    head_dim = width // HEADS
    g = lax.axis_index("group")
    member = lax.axis_index("member")
    z = member // rows
    x = lax.rem(member, rows)

    def at(group, line, row):
        return {"group": group, "member": line * rows + row}

    def add(value, step, size):
        return lax.rem(value + step, size)

    panel = pltpu.make_async_copy(kv_hbm, kv, kv_sem)
    panel.start()
    barrier = pltpu.get_barrier_semaphore()
    peers = [(t, dz, 0) for t in range(groups) for dz in range(lines) if t or dz]
    peers += [(0, 0, dx) for dx in range(1, rows)]
    for t, dz, dx in peers:
        pl.semaphore_signal(
            barrier,
            inc=1,
            device_id=at(add(g, t, groups), add(z, dz, lines), add(x, dx, rows)),
            device_id_type=pl.DeviceIdType.MESH,
        )
    pl.semaphore_wait(barrier, len(peers))

    def ready(ref, sem):
        pltpu.make_async_copy(ref, ref, sem).wait()

    def remote(src, dst, send, recv, device):
        return pltpu.make_async_remote_copy(
            src_ref=src,
            dst_ref=dst,
            send_sem=send,
            recv_sem=recv,
            device_id=device,
            device_id_type=pl.DeviceIdType.MESH,
        )

    def direct(u):
        return lax.rem(u, 2) == 1

    mate = z + 1 - 2 * lax.rem(z, 2)

    def scatter_queries(u, carry=0):
        t = u // cap
        qown[u] = q_ref[pos_ref[u]]
        for dz in range(lines):
            there = (add(g, t, groups), add(z, dz, lines), x)
            send = lambda: remote(
                qown.at[u], qbuf.at[u, x, z], s1.at[u, dz], r1.at[u, dz], at(*there)
            ).start()
            if dz % 2:
                pl.when(direct(u))(send)
            elif dz:
                send()
            else:
                pl.when(t > 0)(send)
                pl.when(t == 0)(
                    lambda: pltpu.make_async_copy(
                        qown.at[u], qbuf.at[u, x, z], r1.at[u, 0]
                    ).start()
                )
        return carry

    lax.fori_loop(0, min(AHEAD, units), scatter_queries, 0)

    def forward(u):
        for dz in range(lines):
            def pass_on():
                line = add(z, lines - dz, lines)
                ready(qbuf.at[u, x, line], r1.at[u, dz])
                for dx in range(1, rows):
                    remote(
                        qbuf.at[u, x, line],
                        qbuf.at[u, x, line],
                        s2.at[u, dx, dz],
                        r2.at[u, dx, dz],
                        at(g, z, add(x, dx, rows)),
                    ).start()

            if dz % 2:
                pl.when(direct(u))(pass_on)
            else:
                pass_on()

    def crossed(u, dz):
        for dx in range(1, rows):
            line = add(z, lines - dz, lines)
            ready(qbuf.at[u, add(x, rows - dx, rows), line], r2.at[u, dx, dz])

    def swap(u):
        for dz in range(0, lines, 2):
            line = add(z, lines - dz, lines)
            crossed(u, dz)
            remote(
                qbuf.at[u, :, line],
                qbuf.at[u, :, line],
                s5.at[u, dz],
                r5.at[u, dz],
                at(g, mate, x),
            ).start()

    def gathered(u):
        def whole():
            for dz in range(lines):
                crossed(u, dz)

        def halves():
            for dz in range(0, lines, 2):
                ready(qbuf.at[u, :, add(mate, lines - dz, lines)], r5.at[u, dz])

        pl.when(direct(u))(whole)
        pl.when(jnp.logical_not(direct(u)))(halves)

    def attend(u):
        gathered(u)
        slot = slot_ref[u]
        live = blocks_ref[cache_ref[g * units + slot]] * BLK
        limit = live - member * count
        share = 1.0 / jnp.full((8, head_dim), live, jnp.int32).astype(jnp.float32)
        share = share[0:1, :]
        keep = lax.broadcasted_iota(jnp.int32, (count, head_dim), 0) < limit
        keep = keep.astype(jnp.float32)
        for h in range(HEADS):
            cols = slice(h * head_dim, (h + 1) * head_dim)
            vals = slice(width + h * head_dim, width + (h + 1) * head_dim)
            q = qbuf[u, :, :, :, cols].reshape(rows * lines * cands, head_dim)
            k = kv[slot, :, cols]
            v = (kv[slot, :, vals].astype(jnp.float32) * keep).astype(jnp.bfloat16)
            score = lax.dot_general(
                q, k, (((1,), (1,)), ((), ())), preferred_element_type=jnp.float32
            )
            half = score * (0.5 * head_dim**-0.5)
            weight = (half + half * jnp.tanh(half)).astype(jnp.bfloat16)
            part = jnp.dot(weight, v, preferred_element_type=jnp.float32) * share
            pbuf[u, :, :, :, cols] = part.astype(jnp.bfloat16).reshape(
                rows, lines, cands, head_dim
            )
        for dx in range(1, rows):
            row = add(x, dx, rows)
            remote(
                pbuf.at[u, row], prec.at[u, dx], s3.at[u, dx], r3.at[u, dx], at(g, z, row)
            ).start()

    def give_back(u):
        t = u // cap
        for dx in range(1, rows):
            ready(prec.at[u, dx], r3.at[u, dx])
        total = pbuf[u, x].astype(jnp.float32)
        for dx in range(1, rows):
            total = total + prec[u, dx].astype(jnp.float32)
        ssum[u] = total.astype(jnp.bfloat16)
        for dz in range(lines):
            line = add(z, dz, lines)
            there = (add(g, groups - t, groups), line, x)
            send = lambda: remote(
                ssum.at[u, line], fin.at[u, dz], s4.at[u, dz], r4.at[u, dz], at(*there)
            ).start()
            if dz:
                send()
            else:
                pl.when(t > 0)(send)
                pl.when(t == 0)(
                    lambda: pltpu.make_async_copy(
                        ssum.at[u, line], fin.at[u, 0], r4.at[u, 0]
                    ).start()
                )

    def later(u):
        scatter_queries(u)

    def stage(i, carry):
        pl.when(i < units)(lambda: forward(i))
        pl.when(i + AHEAD < units)(lambda: later(i + AHEAD))
        pl.when(i == 1)(panel.wait)
        pl.when((i >= 1) & (i < units + 1) & (lax.rem(i, 2) == 1))(lambda: swap(i - 1))
        pl.when((i >= 2) & (i < units + 2))(lambda: attend(i - 2))
        pl.when(i >= 3)(lambda: give_back(i - 3))
        return carry

    lax.fori_loop(0, units + 3, stage, 0)

    def arrived(u, carry):
        for dz in range(lines):
            ready(fin.at[u, dz], r4.at[u, dz])
        return carry

    lax.fori_loop(0, units, arrived, 0)

    def collect(p, carry):
        u = unit_ref[g * units + p]
        total = fin[u, 0].astype(jnp.float32)
        for dz in range(1, lines):
            total = total + fin[u, dz].astype(jnp.float32)
        out_ref[p] = layer_norm(total)
        return carry

    lax.fori_loop(0, units, collect, 0)

    def drain(u, carry):
        t = u // cap
        for dz in range(lines):
            line = add(z, lines - dz, lines)

            def sent():
                ready(qown.at[u], s1.at[u, dz])

            def passed():
                for dx in range(1, rows):
                    ready(qbuf.at[u, x, line], s2.at[u, dx, dz])

            def returned():
                ready(ssum.at[u, add(z, dz, lines)], s4.at[u, dz])

            if dz % 2:
                pl.when(direct(u))(sent)
                pl.when(direct(u))(passed)
            else:
                if dz:
                    sent()
                else:
                    pl.when(t > 0)(sent)
                passed()
                pl.when(jnp.logical_not(direct(u)))(
                    lambda: ready(qbuf.at[u, :, line], s5.at[u, dz])
                )
            if dz:
                returned()
            else:
                pl.when(t > 0)(returned)
        for dx in range(1, rows):
            ready(pbuf.at[u, add(x, dx, rows)], s3.at[u, dx])
        return carry

    lax.fori_loop(0, units, drain, 0)


def exchange(routes, queries, kv_cache, groups, members):
    units, cands, width = queries.shape
    lines = LINE
    rows = members // lines
    cap = units // groups
    count = kv_cache.shape[1]
    smem = pl.BlockSpec(memory_space=pltpu.SMEM)
    vmem = pl.BlockSpec(memory_space=pltpu.VMEM)
    sixteen = jnp.bfloat16
    sem = pltpu.SemaphoreType.DMA
    return pl.pallas_call(
        functools.partial(kernel, (groups, lines, rows, cap)),
        out_shape=jax.ShapeDtypeStruct(queries.shape, jnp.float32),
        in_specs=[smem] * 5 + [vmem, pl.BlockSpec(memory_space=pl.ANY)],
        out_specs=vmem,
        scratch_shapes=[
            pltpu.VMEM(queries.shape, sixteen),
            pltpu.VMEM(kv_cache.shape, sixteen),
            pltpu.VMEM((units, rows, lines, cands, width), sixteen),
            pltpu.VMEM((units, rows, lines, cands, width), sixteen),
            pltpu.VMEM((units, rows, lines, cands, width), sixteen),
            pltpu.VMEM((units, lines, cands, width), sixteen),
            pltpu.VMEM((units, lines, cands, width), sixteen),
            sem,
            sem((units, lines)),
            sem((units, lines)),
            sem((units, rows, lines)),
            sem((units, rows, lines)),
            sem((units, rows)),
            sem((units, rows)),
            sem((units, lines)),
            sem((units, lines)),
            sem((units, lines)),
            sem((units, lines)),
        ],
        compiler_params=pltpu.CompilerParams(
            collective_id=0, has_side_effects=True, vmem_limit_bytes=56 * 1024 * 1024
        ),
        cost_estimate=pl.CostEstimate(
            flops=4 * units * cands * members * count * width,
            bytes_accessed=2 * kv_cache.size,
            transcendentals=units * cands * members * count * HEADS,
        ),
    )(*routes, queries, kv_cache)


def on_device(candidates, kv_cache, cache_request, rank_request, hist_blocks, w_uq, w_out):
    groups = lax.axis_size("group")
    per_group = kv_cache.shape[0]
    cand_rows = candidates.shape[0]
    width = candidates.shape[2]
    group_now = lax.axis_index("group")
    members = lax.axis_size("member")
    routes = routing(cache_request, rank_request, per_group, groups, group_now)
    routes += (cache_request, hist_blocks)
    inputs = jnp.transpose(candidates, (1, 0, 2)).astype(jnp.float32)
    normed = layer_norm(inputs).astype(jnp.bfloat16).reshape(per_group * cand_rows, width)
    projected = jax.nn.silu(jnp.dot(normed, w_uq, preferred_element_type=jnp.float32))
    gates = projected[:, :width].reshape(per_group, cand_rows, width)
    queries = projected[:, width:].astype(jnp.bfloat16).reshape(per_group, cand_rows, width)
    attn = exchange(routes, queries, kv_cache, groups, members)
    gated = (attn * gates).astype(jnp.bfloat16).reshape(cand_rows * per_group, width)
    result = jnp.dot(gated, w_out, preferred_element_type=jnp.float32) + inputs.reshape(
        cand_rows * per_group, width
    )
    result = result.astype(jnp.bfloat16).reshape(per_group, cand_rows, width)
    return jnp.transpose(result, (1, 0, 2))


def solution(mesh):
    return jax.shard_map(
        on_device,
        mesh=mesh,
        in_specs=(P("member", "group", None), P("group", "member", None), P(), P(), P(), P(), P()),
        out_specs=P("member", "group", None),
        check_vma=False,
    )
```

```python
import functools

import jax
import jax.numpy as jnp
from jax import lax
from jax.experimental import pallas as pl
from jax.experimental.pallas import tpu as pltpu
from jax.sharding import PartitionSpec as P

HEADS = 8
BLK = 128
LINE = 4
AHEAD = 3


def layer_norm(values):
    center = values - jnp.mean(values, axis=-1, keepdims=True)
    spread = jnp.mean(center * center, axis=-1, keepdims=True)
    return center * lax.rsqrt(spread + 1e-05)


def routing(cache_request, rank_request, per_group, groups, group_now):
    cap = per_group // groups
    first = group_now * per_group
    slot_ids = jnp.arange(cache_request.shape[0], dtype=jnp.int32)
    match = cache_request[:, None] == rank_request[None, :]
    rank_pos = jnp.sum(jnp.where(match, slot_ids[None, :], 0), axis=1)
    target = rank_pos // per_group
    owner_grp = slot_ids // per_group
    earlier = (
        (owner_grp[:, None] == owner_grp[None, :])
        & (target[:, None] == target[None, :])
        & (slot_ids[None, :] < slot_ids[:, None])
    )
    arrival = jnp.sum(earlier.astype(jnp.int32), axis=1)
    leaving = lax.rem(owner_grp - group_now + groups, groups) * cap + arrival
    arriving = lax.rem(group_now - target + groups, groups) * cap + arrival
    ids = jnp.arange(per_group, dtype=jnp.int32)
    unit_of_pos = jnp.sum(jnp.where(match, leaving[:, None], 0), axis=0)
    ranks = (target == group_now)[:, None] & (leaving[:, None] == ids[None, :])
    pos_of_unit = jnp.sum(jnp.where(ranks, (rank_pos - first)[:, None], 0), axis=0)
    holds = (owner_grp == group_now)[:, None] & (arriving[:, None] == ids[None, :])
    slot_of_unit = jnp.sum(jnp.where(holds, (slot_ids - first)[:, None], 0), axis=0)
    return pos_of_unit, unit_of_pos, slot_of_unit


def kernel(
    dims,
    pos_ref,
    unit_ref,
    slot_ref,
    cache_ref,
    blocks_ref,
    q_ref,
    kv_hbm,
    out_ref,
    qown,
    kv,
    qbuf,
    pbuf,
    prec,
    ssum,
    fin,
    kv_sem,
    s1,
    r1,
    s2,
    r2,
    s3,
    r3,
    s4,
    r4,
    s5,
    r5,
):
    groups, lines, rows, cap = dims
    units = groups * cap
    cands, width = q_ref.shape[1:]
    count = kv_hbm.shape[1]
    head_dim = width // HEADS
    g = lax.axis_index("group")
    member = lax.axis_index("member")
    z = member // rows
    x = lax.rem(member, rows)

    def at(group, line, row):
        return {"group": group, "member": line * rows + row}

    def add(value, step, size):
        return lax.rem(value + step, size)

    panel = pltpu.make_async_copy(kv_hbm, kv, kv_sem)
    panel.start()
    barrier = pltpu.get_barrier_semaphore()
    peers = [(t, dz, 0) for t in range(groups) for dz in range(lines) if t or dz]
    peers += [(0, 0, dx) for dx in range(1, rows)]
    for t, dz, dx in peers:
        pl.semaphore_signal(
            barrier,
            inc=1,
            device_id=at(add(g, t, groups), add(z, dz, lines), add(x, dx, rows)),
            device_id_type=pl.DeviceIdType.MESH,
        )
    pl.semaphore_wait(barrier, len(peers))

    def ready(ref, sem):
        pltpu.make_async_copy(ref, ref, sem).wait()

    def remote(src, dst, send, recv, device):
        return pltpu.make_async_remote_copy(
            src_ref=src,
            dst_ref=dst,
            send_sem=send,
            recv_sem=recv,
            device_id=device,
            device_id_type=pl.DeviceIdType.MESH,
        )

    def direct(u):
        return lax.rem(u, 2) == 1

    mate = z + 1 - 2 * lax.rem(z, 2)

    def scatter_queries(u, carry=0):
        t = u // cap
        qown[u] = q_ref[pos_ref[u]]
        for dz in range(lines):
            there = (add(g, t, groups), add(z, dz, lines), x)
            send = lambda: remote(
                qown.at[u], qbuf.at[u, x, z], s1.at[u, dz], r1.at[u, dz], at(*there)
            ).start()
            if dz % 2:
                pl.when(direct(u))(send)
            elif dz:
                send()
            else:
                pl.when(t > 0)(send)
                pl.when(t == 0)(
                    lambda: pltpu.make_async_copy(
                        qown.at[u], qbuf.at[u, x, z], r1.at[u, 0]
                    ).start()
                )
        return carry

    lax.fori_loop(0, min(AHEAD, units), scatter_queries, 0)

    def forward(u):
        for dz in range(lines):
            def pass_on():
                line = add(z, lines - dz, lines)
                ready(qbuf.at[u, x, line], r1.at[u, dz])
                for dx in range(1, rows):
                    remote(
                        qbuf.at[u, x, line],
                        qbuf.at[u, x, line],
                        s2.at[u, dx, dz],
                        r2.at[u, dx, dz],
                        at(g, z, add(x, dx, rows)),
                    ).start()

            if dz % 2:
                pl.when(direct(u))(pass_on)
            else:
                pass_on()

    def crossed(u, dz):
        for dx in range(1, rows):
            line = add(z, lines - dz, lines)
            ready(qbuf.at[u, add(x, rows - dx, rows), line], r2.at[u, dx, dz])

    def swap(u):
        for dz in range(0, lines, 2):
            line = add(z, lines - dz, lines)
            crossed(u, dz)
            remote(
                qbuf.at[u, :, line],
                qbuf.at[u, :, line],
                s5.at[u, dz],
                r5.at[u, dz],
                at(g, mate, x),
            ).start()

    def gathered(u):
        def whole():
            for dz in range(lines):
                crossed(u, dz)

        def halves():
            for dz in range(0, lines, 2):
                ready(qbuf.at[u, :, add(mate, lines - dz, lines)], r5.at[u, dz])

        pl.when(direct(u))(whole)
        pl.when(jnp.logical_not(direct(u)))(halves)

    def attend(u):
        gathered(u)
        slot = slot_ref[u]
        live = blocks_ref[cache_ref[g * units + slot]] * BLK
        limit = live - member * count
        share = 1.0 / jnp.full((8, head_dim), live, jnp.int32).astype(jnp.float32)
        share = share[0:1, :]
        keep = lax.broadcasted_iota(jnp.int32, (count, head_dim), 0) < limit
        keep = keep.astype(jnp.float32)
        for h in range(HEADS):
            cols = slice(h * head_dim, (h + 1) * head_dim)
            vals = slice(width + h * head_dim, width + (h + 1) * head_dim)
            q = qbuf[u, :, :, :, cols].reshape(rows * lines * cands, head_dim)
            k = kv[slot, :, cols]
            v = (kv[slot, :, vals].astype(jnp.float32) * keep).astype(jnp.bfloat16)
            score = lax.dot_general(
                q, k, (((1,), (1,)), ((), ())), preferred_element_type=jnp.float32
            )
            half = score * (0.5 * head_dim**-0.5)
            weight = (half + half * jnp.tanh(half)).astype(jnp.bfloat16)
            part = jnp.dot(weight, v, preferred_element_type=jnp.float32) * share
            pbuf[u, :, :, :, cols] = part.astype(jnp.bfloat16).reshape(
                rows, lines, cands, head_dim
            )
        for dx in range(1, rows):
            row = add(x, dx, rows)
            remote(
                pbuf.at[u, row], prec.at[u, dx], s3.at[u, dx], r3.at[u, dx], at(g, z, row)
            ).start()

    def give_back(u):
        t = u // cap
        for dx in range(1, rows):
            ready(prec.at[u, dx], r3.at[u, dx])
        total = pbuf[u, x].astype(jnp.float32)
        for dx in range(1, rows):
            total = total + prec[u, dx].astype(jnp.float32)
        ssum[u] = total.astype(jnp.bfloat16)
        for dz in range(lines):
            line = add(z, dz, lines)
            there = (add(g, groups - t, groups), line, x)
            send = lambda: remote(
                ssum.at[u, line], fin.at[u, dz], s4.at[u, dz], r4.at[u, dz], at(*there)
            ).start()
            if dz:
                send()
            else:
                pl.when(t > 0)(send)
                pl.when(t == 0)(
                    lambda: pltpu.make_async_copy(
                        ssum.at[u, line], fin.at[u, 0], r4.at[u, 0]
                    ).start()
                )

    def later(u):
        scatter_queries(u)

    def stage(i, carry):
        pl.when(i < units)(lambda: forward(i))
        pl.when(i + AHEAD < units)(lambda: later(i + AHEAD))
        pl.when(i == 1)(panel.wait)
        pl.when((i >= 2) & (i < units + 2))(lambda: attend(i - 2))
        pl.when((i >= 1) & (i < units + 1) & (lax.rem(i, 2) == 1))(lambda: swap(i - 1))
        pl.when(i >= 3)(lambda: give_back(i - 3))
        return carry

    lax.fori_loop(0, units + 3, stage, 0)

    def arrived(u, carry):
        for dz in range(lines):
            ready(fin.at[u, dz], r4.at[u, dz])
        return carry

    lax.fori_loop(0, units, arrived, 0)

    def collect(p, carry):
        u = unit_ref[g * units + p]
        total = fin[u, 0].astype(jnp.float32)
        for dz in range(1, lines):
            total = total + fin[u, dz].astype(jnp.float32)
        out_ref[p] = layer_norm(total)
        return carry

    lax.fori_loop(0, units, collect, 0)

    def drain(u, carry):
        t = u // cap
        for dz in range(lines):
            line = add(z, lines - dz, lines)

            def sent():
                ready(qown.at[u], s1.at[u, dz])

            def passed():
                for dx in range(1, rows):
                    ready(qbuf.at[u, x, line], s2.at[u, dx, dz])

            def returned():
                ready(ssum.at[u, add(z, dz, lines)], s4.at[u, dz])

            if dz % 2:
                pl.when(direct(u))(sent)
                pl.when(direct(u))(passed)
            else:
                if dz:
                    sent()
                else:
                    pl.when(t > 0)(sent)
                passed()
                pl.when(jnp.logical_not(direct(u)))(
                    lambda: ready(qbuf.at[u, :, line], s5.at[u, dz])
                )
            if dz:
                returned()
            else:
                pl.when(t > 0)(returned)
        for dx in range(1, rows):
            ready(pbuf.at[u, add(x, dx, rows)], s3.at[u, dx])
        return carry

    lax.fori_loop(0, units, drain, 0)


def exchange(routes, queries, kv_cache, groups, members):
    units, cands, width = queries.shape
    lines = LINE
    rows = members // lines
    cap = units // groups
    count = kv_cache.shape[1]
    smem = pl.BlockSpec(memory_space=pltpu.SMEM)
    vmem = pl.BlockSpec(memory_space=pltpu.VMEM)
    sixteen = jnp.bfloat16
    sem = pltpu.SemaphoreType.DMA
    return pl.pallas_call(
        functools.partial(kernel, (groups, lines, rows, cap)),
        out_shape=jax.ShapeDtypeStruct(queries.shape, jnp.float32),
        in_specs=[smem] * 5 + [vmem, pl.BlockSpec(memory_space=pl.ANY)],
        out_specs=vmem,
        scratch_shapes=[
            pltpu.VMEM(queries.shape, sixteen),
            pltpu.VMEM(kv_cache.shape, sixteen),
            pltpu.VMEM((units, rows, lines, cands, width), sixteen),
            pltpu.VMEM((units, rows, lines, cands, width), sixteen),
            pltpu.VMEM((units, rows, lines, cands, width), sixteen),
            pltpu.VMEM((units, lines, cands, width), sixteen),
            pltpu.VMEM((units, lines, cands, width), sixteen),
            sem,
            sem((units, lines)),
            sem((units, lines)),
            sem((units, rows, lines)),
            sem((units, rows, lines)),
            sem((units, rows)),
            sem((units, rows)),
            sem((units, lines)),
            sem((units, lines)),
            sem((units, lines)),
            sem((units, lines)),
        ],
        compiler_params=pltpu.CompilerParams(
            collective_id=0, has_side_effects=True, vmem_limit_bytes=56 * 1024 * 1024
        ),
        cost_estimate=pl.CostEstimate(
            flops=4 * units * cands * members * count * width,
            bytes_accessed=2 * kv_cache.size,
            transcendentals=units * cands * members * count * HEADS,
        ),
    )(*routes, queries, kv_cache)


def on_device(candidates, kv_cache, cache_request, rank_request, hist_blocks, w_uq, w_out):
    groups = lax.axis_size("group")
    per_group = kv_cache.shape[0]
    cand_rows = candidates.shape[0]
    width = candidates.shape[2]
    group_now = lax.axis_index("group")
    members = lax.axis_size("member")
    routes = routing(cache_request, rank_request, per_group, groups, group_now)
    routes += (cache_request, hist_blocks)
    inputs = jnp.transpose(candidates, (1, 0, 2)).astype(jnp.float32)
    normed = layer_norm(inputs).astype(jnp.bfloat16).reshape(per_group * cand_rows, width)
    projected = jax.nn.silu(jnp.dot(normed, w_uq, preferred_element_type=jnp.float32))
    gates = projected[:, :width].reshape(per_group, cand_rows, width)
    queries = projected[:, width:].astype(jnp.bfloat16).reshape(per_group, cand_rows, width)
    attn = exchange(routes, queries, kv_cache, groups, members)
    gated = (attn * gates).astype(jnp.bfloat16).reshape(cand_rows * per_group, width)
    result = jnp.dot(gated, w_out, preferred_element_type=jnp.float32) + inputs.reshape(
        cand_rows * per_group, width
    )
    result = result.astype(jnp.bfloat16).reshape(per_group, cand_rows, width)
    return jnp.transpose(result, (1, 0, 2))


def solution(mesh):
    return jax.shard_map(
        on_device,
        mesh=mesh,
        in_specs=(P("member", "group", None), P("group", "member", None), P(), P(), P(), P(), P()),
        out_specs=P("member", "group", None),
        check_vma=False,
    )
```
